32 devices in a mesh: dp: 8 (over z, x), tensor: 4 (over y, core).
Axes of the slice: x: 2, y: 2, z: 4, core: 2. Of those that a mesh axis runs over, the one named last changes fastest.
Arguments:
- tokens: bfloat16 [24576, 1024], P('dp'), may hold values from -6 to 6
- starts: int32 [24576], P('dp'), may hold values from 0 to 1, as said below
- norm_gains: float32 [2, 1024], replicated, may hold values from 0.1 to 1.9
- in_weight: bfloat16 [3, 1024, 1024], P(None, None, 'tensor'), may hold values from -0.1875 to 0.1875
- conv_weight: float32 [3, 1024], P(None, 'tensor'), may hold values from -3 to 3
- out_weight: bfloat16 [1024, 1024], P('tensor'), may hold values from -0.1875 to 0.1875
- ffn_weight: bfloat16 [2, 1024, 4608], P(None, None, 'tensor'), may hold values from -0.1875 to 0.1875
- down_weight: bfloat16 [4608, 1024], P('tensor'), may hold values from -0.1875 to 0.1875
- cotangent: bfloat16 [24576, 1024], P('dp'), may hold values from -6 to 6
Outputs:
- block_out: bfloat16 [24576, 1024], P(('dp', 'tensor'))
- grad_tokens: float32 [24576, 1024], P(('dp', 'tensor'))
- grad_gains: float32 [2, 1024], replicated
- grad_in_weight: float32 [3, 1024, 1024], P(None, 'dp', 'tensor')
- grad_conv: float32 [3, 1024], replicated
- grad_out_weight: float32 [1024, 1024], P('tensor', 'dp')
- grad_ffn: float32 [2, 1024, 4608], P(None, 'dp', 'tensor')
- grad_down: float32 [4608, 1024], P('tensor', 'dp')
The draws below stay inside these ranges and needn't reach their ends.
Inputs may be any that keep to these rules, and one draw needn't show every extreme that they name: starts[0], starts[3071] and starts[21505] are 1, and starts is 0 at every token between the last two, so one document runs from token 3071 to token 21504; further documents may begin anywhere among the first 3071 tokens and the last 3070.
All inputs are finite; a program needn't handle non-finite values.
Results may differ from the reference program's by a relative error of at most 0.024.
Values may be sent and summed in bfloat16 or wider, within the bound.
No kernel may reach another device: no remote copies, remote signals or barrier semaphores. Data moves between devices by JAX's collectives and lax.ppermute only.
A program may use at most 256 MiB of HBM per device.

```python
import math
import jax
import jax.numpy as jnp
from jax import lax

D = 1024
FF = 4608
TOK_DEV = 3072
TOKENS = 24576


def draw_starts(key, part):
    key = jax.random.fold_in(key, 7)
    position = jnp.arange(TOKENS)
    first_edge = TOK_DEV - 1
    last_edge = TOKENS - TOK_DEV + 1
    near_ends = (position < first_edge) | (position > last_edge)
    random_pick = jax.random.randint(key, (TOKENS,), 0, 6) == 0
    flags = jnp.where(near_ends & random_pick, 1, 0)
    forced = (position == 0) | (position == first_edge) | (position == last_edge)
    flags = jnp.where(forced, 1, flags)
    return flags.astype(jnp.int32)


def levels(stream_key, shape, shards, low, largest):
    def one(axis_at, parts):
        steps = jax.random.uniform(jax.random.fold_in(jax.random.fold_in(stream_key, 6), axis_at), (parts,), jnp.float32, low / len(shards), largest / len(shards))
        return jnp.repeat(jnp.exp(steps), shape[axis_at] // parts).reshape((-1,) + (1,) * (len(shape) - axis_at - 1))

    factor_of = one(*shards[0])
    for cut in shards[1:]:
        factor_of = factor_of * one(*cut)
    return factor_of


def centred(stream_key, extent, width, reach, cuts=(), kind=jnp.bfloat16):
    entries = jax.random.normal(stream_key, extent, jnp.float32) * width
    if len(cuts) > 0:
        entries = levels(stream_key, extent, cuts, -0.22, 0.18) * entries
    return jnp.clip(entries, min=-reach, max=reach).astype(kind)


def setup_inputs(seed: int = 0) -> dict:
    seeds = jax.random.split(jax.random.key(seed), 10)
    tokens = centred(seeds[0], (TOKENS, D), 1.0, 6.0, ((0, 8),))
    starts = draw_starts(jax.random.fold_in(seeds[9], 71), 0)
    norm_gains = jnp.clip(1.0 + 0.18 * jax.random.normal(seeds[2], (2, D), jnp.float32), 0.1, 1.9)
    in_weight = centred(seeds[3], (3, D, D), D ** -0.5, 0.1875, ((2, 4),))
    conv_weight = centred(seeds[4], (3, D), 0.6, 3.0, ((1, 4),), jnp.float32)
    out_weight = centred(seeds[5], (D, D), D ** -0.5, 0.1875, ((0, 4),))
    ffn_weight = centred(seeds[6], (2, D, FF), D ** -0.5, 0.1875, ((2, 4),))
    down_weight = centred(seeds[7], (FF, D), (FF // 4) ** -0.5, 0.1875, ((0, 4),))
    cotangent = centred(seeds[8], (TOKENS, D), 1.0, 6.0, ((0, 8),))
    return {"tokens": tokens, "starts": starts, "norm_gains": norm_gains, "in_weight": in_weight, "conv_weight": conv_weight, "out_weight": out_weight, "ffn_weight": ffn_weight, "down_weight": down_weight, "cotangent": cotangent}


EPSILON = 1e-05

@jax.custom_vjp
def low(v):
    return lax.optimization_barrier(v.astype(jnp.bfloat16)).astype(jnp.float32)

@jax.custom_vjp
def low_back(v):
    return v

def low_keep(v):
    return (low(v), None)

def low_pass(kept, grad):
    return (grad,)

def back_keep(v):
    return (v, None)

def back_low(kept, grad):
    return (low(grad),)
low.defvjp(low_keep, low_pass)
low_back.defvjp(back_keep, back_low)

def rms_scale(values, gain):
    return values * lax.rsqrt(lax.optimization_barrier(jnp.mean(values * values, axis=-1, keepdims=True)) + EPSILON) * gain

def forward(tokens, norm_gains, in_weight, conv_weight, out_weight, ffn_weight, down_weight, keep_mask):
    block_rows = math.gcd(TOKENS, 1024)
    block_count = TOKENS // block_rows
    highest = lax.Precision.HIGHEST

    def first_section(x_block):
        normed_in = low(rms_scale(x_block, norm_gains[0]))
        projected = low_back(jnp.einsum('td,kde->kte', normed_in, in_weight, precision=highest))
        return (low(projected[0] * projected[2]), projected[1])
    mixed, c_gate = lax.map(jax.checkpoint(first_section), tokens.reshape(block_count, block_rows, D))
    mixed = mixed.reshape(TOKENS, D)
    c_gate = c_gate.reshape(TOKENS, D)
    prev_one = jnp.concatenate([jnp.zeros((1, D), jnp.float32), mixed[:-1]], 0)
    prev_two = jnp.concatenate([jnp.zeros((2, D), jnp.float32), mixed[:-2]], 0)
    keep_prev = jnp.concatenate([jnp.ones((1,), jnp.float32), keep_mask[:-1]])
    conv_out = conv_weight[2] * mixed + keep_mask[:, None] * (conv_weight[1] * prev_one + conv_weight[0] * keep_prev[:, None] * prev_two)

    def second_section(pieces):
        x_block, conv_block, gate_block = pieces
        gated_mix = low(gate_block * conv_block)
        mixer_out = low_back(jnp.dot(gated_mix, out_weight, precision=highest))
        resid = x_block + mixer_out
        normed_ffn = low(rms_scale(resid, norm_gains[1]))
        gate_up = low_back(jnp.einsum('td,kdf->ktf', normed_ffn, ffn_weight, precision=highest))
        activation = low(jax.nn.silu(gate_up[0]) * gate_up[1])
        return resid + jnp.dot(activation, down_weight, precision=highest)
    result = lax.map(jax.checkpoint(second_section), (tokens.reshape(block_count, block_rows, D), conv_out.reshape(block_count, block_rows, D), c_gate.reshape(block_count, block_rows, D)))
    return result.reshape(TOKENS, D)

def reference(tokens, starts, norm_gains, in_weight, conv_weight, out_weight, ffn_weight, down_weight, cotangent):
    keep_mask = 1.0 - starts.astype(jnp.float32)

    def run_block(x_vals, gain_vals, in_vals, conv_vals, out_vals, ffn_vals, down_vals):
        return forward(x_vals, gain_vals, in_vals, conv_vals, out_vals, ffn_vals, down_vals, keep_mask)
    result, pullback = jax.vjp(run_block, tokens.astype(jnp.float32), norm_gains.astype(jnp.float32), in_weight.astype(jnp.float32), conv_weight.astype(jnp.float32), out_weight.astype(jnp.float32), ffn_weight.astype(jnp.float32), down_weight.astype(jnp.float32))
    grads = pullback(cotangent.astype(jnp.float32))
    return (result.astype(jnp.bfloat16), grads[0], grads[1], grads[2], grads[3], grads[4], grads[5], grads[6])
```

```python
import jax
import jax.numpy as jnp
from jax import lax
from jax.sharding import PartitionSpec as P

EPSILON = 1e-05
F32 = jnp.float32
BF16 = jnp.bfloat16


def swap(value, axis, bits):
    peers = lax.axis_size(axis)
    return lax.ppermute(value, axis, [(i, i ^ bits) for i in range(peers)])


def shift(value, axes, by):
    peers = lax.axis_size(axes)
    return lax.ppermute(value, axes, [(i, i + by) for i in range(peers) if 0 <= i + by < peers])


def gather_pieces(value):
    count = lax.axis_size("tensor")
    pieces = [value] + [None] * (count - 1)
    pieces[1] = swap(value, "tensor", 1)
    for k in range(2, count, 2):
        pieces[k] = swap(value, "tensor", k)
        pieces[k + 1] = swap(pieces[k], "tensor", 1)
    return pieces


def add_low(mine, received):
    return (mine.astype(F32) + received.astype(F32)).astype(BF16)


def scatter_pieces(pieces):
    count = len(pieces)
    evens = [
        add_low(pieces[k], swap(pieces[k + 1], "tensor", 1)) for k in range(0, count, 2)
    ]
    total = evens[0].astype(F32)
    for k in range(2, count, 2):
        total = total + swap(evens[k // 2], "tensor", k).astype(F32)
    return total


def scatter_dp(value):
    count = lax.axis_size("dp")
    index = lax.axis_index("dp")
    bits = 1
    while bits < count:
        side = (index // bits) % 2
        pairs = value.reshape((value.shape[0] // 2, 2) + value.shape[1:])
        sent = lax.dynamic_index_in_dim(pairs, 1 - side, 1, keepdims=False)
        kept = lax.dynamic_index_in_dim(pairs, side, 1, keepdims=False)
        received = swap(sent, "dp", bits)
        value = kept.astype(F32) + received.astype(F32)
        bits *= 2
        if bits < count:
            value = value.astype(BF16)
    return value[0]


def sum_all(value):
    for axis in ("tensor", "dp"):
        bits = 1
        while bits < lax.axis_size(axis):
            value = value + swap(value, axis, bits)
            bits *= 2
    return value


def inverse_rms(values):
    return lax.rsqrt(jnp.mean(values * values, axis=-1, keepdims=True) + EPSILON)


def norm_backward(grad_normed, normed, inverse, gain):
    scaled = grad_normed * gain
    return inverse * (scaled - normed * jnp.mean(scaled * normed, axis=-1, keepdims=True))


def matmul(a, b, dims):
    return lax.dot_general(a, b, (dims, ((), ())), preferred_element_type=F32)


def to_owners(value):
    count = lax.axis_size("tensor")
    here = lax.axis_index("tensor")
    channels = value.shape[1] // count
    result = jnp.zeros(value.shape, value.dtype)
    for k in range(count):
        block = value[:, k * channels : (k + 1) * channels]
        result = lax.dynamic_update_slice(result, block, (0, (here ^ k) * channels))
    return result


def from_owners(value):
    count = lax.axis_size("tensor")
    here = lax.axis_index("tensor")
    channels = value.shape[1] // count
    return jnp.concatenate(
        [lax.dynamic_slice_in_dim(value, (here ^ k) * channels, channels, 1) for k in range(count)], 1
    )


HEAD = 16


def body(
    tokens,
    starts,
    norm_gains,
    in_weight,
    conv_weight,
    out_weight,
    ffn_weight,
    down_weight,
    cotangent,
):
    row_count, width = tokens.shape
    count = lax.axis_size("tensor")
    dp_count = lax.axis_size("dp")
    here = lax.axis_index("tensor")
    rows = row_count // count
    first = here * rows

    keep_all = 1.0 - starts.astype(F32)
    edge = jnp.concatenate(
        [tokens[-HEAD:], jnp.broadcast_to(keep_all[-1], (HEAD, width)).astype(BF16)], 0
    )
    before = shift(edge, "dp", 1)
    back = jnp.maximum(first - HEAD, 0)
    head_rows = jnp.where(
        here == 0, before[:HEAD], lax.dynamic_slice_in_dim(tokens, back, HEAD, 0)
    )
    keep_prev = jnp.where(
        here == 0, before[HEAD, 0].astype(F32), lax.dynamic_index_in_dim(keep_all, jnp.maximum(first - 1, 0), 0, False)
    )
    keep = lax.dynamic_slice_in_dim(keep_all, first, rows, 0)
    keep_before = jnp.concatenate([keep_prev[None], keep[:-1]])[:, None]
    keep_after = jnp.concatenate([keep[1:], jnp.ones((1,), F32)])[:, None]
    keep = keep[:, None]

    in_pieces = gather_pieces(in_weight)
    out_pieces = gather_pieces(out_weight)
    conv_pieces = gather_pieces(conv_weight)
    in_full = jnp.concatenate(in_pieces, 2)
    out_full = jnp.concatenate(out_pieces, 0)
    conv = jnp.concatenate(conv_pieces, 1)

    x_share = lax.dynamic_slice_in_dim(tokens, first, rows, 0)
    x_ext = jnp.concatenate([head_rows, x_share], 0).astype(F32)
    inverse_ext = inverse_rms(x_ext)
    normed_ext = x_ext * inverse_ext
    nin_ext = (normed_ext * norm_gains[0]).astype(BF16)
    x = x_ext[HEAD:]
    inverse_one = inverse_ext[HEAD:]
    x_normed = normed_ext[HEAD:]
    normed_in = nin_ext[HEAD:]
    proj_b = matmul(nin_ext, in_full[0], ((1,), (0,)))
    proj_x = matmul(nin_ext, in_full[2], ((1,), (0,)))
    proj_c = matmul(normed_in, in_full[1], ((1,), (0,)))
    mixed_ext = (proj_b * proj_x).astype(BF16).astype(F32)
    mixed = mixed_ext[HEAD:]
    prev_one = mixed_ext[HEAD - 1 : -1]
    prev_two = keep_before * mixed_ext[HEAD - 2 : -2]
    conv_out = conv[2] * mixed + keep * (conv[1] * prev_one + conv[0] * prev_two)
    gated_mix = (proj_c * conv_out).astype(BF16)
    resid = x + matmul(gated_mix, out_full, ((1,), (0,)))
    inverse_two = inverse_rms(resid)
    resid_normed = resid * inverse_two
    normed_ffn = (resid_normed * norm_gains[1]).astype(BF16)

    nf_pieces = gather_pieces(normed_ffn)
    block_pieces = []
    dnf_pieces = []
    grad_gate = grad_up = grad_down = 0.0
    for pair in range(0, count, 2):
        nf = jnp.concatenate(nf_pieces[pair : pair + 2], 0)
        g = jnp.concatenate(
            [
                lax.dynamic_slice_in_dim(cotangent, (here ^ k) * rows, rows, 0)
                for k in (pair, pair + 1)
            ],
            0,
        )
        gate = matmul(nf, ffn_weight[0], ((1,), (0,)))
        up = matmul(nf, ffn_weight[1], ((1,), (0,)))
        sigmoid = jax.nn.sigmoid(gate)
        silu = gate * sigmoid
        act = (silu * up).astype(BF16)
        d_act = matmul(g, down_weight, ((1,), (1,)))
        d_gate = (d_act * up * sigmoid * (1.0 + gate * (1.0 - sigmoid))).astype(BF16)
        d_up = (d_act * silu).astype(BF16)
        block = matmul(act, down_weight, ((1,), (0,))).astype(BF16)
        d_nf = (
            matmul(d_gate, ffn_weight[0], ((1,), (1,)))
            + matmul(d_up, ffn_weight[1], ((1,), (1,)))
        ).astype(BF16)
        block_pieces += [block[:rows], block[rows:]]
        dnf_pieces += [d_nf[:rows], d_nf[rows:]]
        grad_gate = grad_gate + matmul(nf, d_gate, ((0,), (0,)))
        grad_up = grad_up + matmul(nf, d_up, ((0,), (0,)))
        grad_down = grad_down + matmul(g, act, ((0,), (0,)))

    d_nf = scatter_pieces(dnf_pieces)
    split = (dp_count, width // dp_count, -1)
    out_gate, out_up, out_down = [
        scatter_dp(value.astype(BF16).reshape(split)) for value in (grad_gate, grad_up, grad_down)
    ]
    block_out = (resid + scatter_pieces(block_pieces)).astype(BF16)

    g_share = lax.dynamic_slice_in_dim(cotangent, first, rows, 0).astype(F32)
    d_res = g_share + norm_backward(d_nf, resid_normed, inverse_two, norm_gains[1])
    d_res_low = d_res.astype(BF16)
    gain_two = jnp.sum(d_nf * resid_normed, axis=0)
    d_gated = matmul(d_res_low, out_full, ((1,), (1,)))
    grad_out = matmul(d_res_low, gated_mix, ((0,), (0,))).astype(BF16)
    d_cgate = d_gated * conv_out
    d_conv = d_gated * proj_c
    weighted = keep * d_conv
    edge_back = jnp.stack([weighted[0], keep[0] * weighted[1]])
    after = from_owners(shift(to_owners(edge_back), ("dp", "tensor"), -1))
    next_one = jnp.concatenate([weighted[1:], after[0:1]], 0)
    next_two = jnp.concatenate(
        [keep_after[:-2] * weighted[2:], keep_after[-2:-1] * after[0:1], after[1:2]], 0
    )
    d_mixed = conv[2] * d_conv + conv[1] * next_one + conv[0] * next_two
    conv_local = jnp.stack(
        [
            jnp.sum(weighted * prev_two, axis=0),
            jnp.sum(weighted * prev_one, axis=0),
            jnp.sum(d_conv * mixed, axis=0),
        ]
    )
    d_proj = [
        (d_mixed * proj_x[HEAD:]).astype(BF16),
        d_cgate.astype(BF16),
        (d_mixed * proj_b[HEAD:]).astype(BF16),
    ]
    d_ni = sum(matmul(d_proj[k], in_full[k], ((1,), (1,))) for k in range(3))
    grad_in = [matmul(normed_in, d_proj[k], ((0,), (0,))).astype(BF16) for k in range(3)]
    grad_tokens = d_res + norm_backward(d_ni, x_normed, inverse_one, norm_gains[0])
    gain_one = jnp.sum(d_ni * x_normed, axis=0)

    mixer = jnp.stack(grad_in + [grad_out])
    channels = width // count
    mixer = [
        mixer[:, :, k * channels : (k + 1) * channels].reshape(4, dp_count, width // dp_count, channels).swapaxes(0, 1)
        for k in range(count)
    ]
    mixer = scatter_dp(scatter_pieces(mixer).astype(BF16))

    conv_order = to_owners(conv_local)
    small = sum_all(jnp.concatenate([jnp.stack([gain_one, gain_two]), conv_order], 0))
    return (
        block_out,
        grad_tokens,
        small[:2],
        mixer[:3],
        small[2:],
        mixer[3].T,
        jnp.stack([out_gate, out_up]),
        out_down.T,
    )


def solution(mesh):
    return jax.shard_map(
        body,
        mesh=mesh,
        in_specs=(
            P("dp", None),
            P("dp"),
            P(),
            P(None, None, "tensor"),
            P(None, "tensor"),
            P("tensor", None),
            P(None, None, "tensor"),
            P("tensor", None),
            P("dp", None),
        ),
        out_specs=(
            P(("dp", "tensor"), None),
            P(("dp", "tensor"), None),
            P(),
            P(None, "dp", "tensor"),
            P(),
            P("tensor", "dp"),
            P(None, "dp", "tensor"),
            P("tensor", "dp"),
        ),
        check_vma=False,
    )
```

```python
import functools

import jax
import jax.numpy as jnp
from jax import lax
from jax.experimental import pallas as pl
from jax.experimental.pallas import tpu as pltpu
from jax.sharding import PartitionSpec as P

EPSILON = 1e-05
F32 = jnp.float32
BF16 = jnp.bfloat16


def swap(value, axis, bits):
    peers = lax.axis_size(axis)
    return lax.ppermute(value, axis, [(i, i ^ bits) for i in range(peers)])


def shift(value, axes, by):
    peers = lax.axis_size(axes)
    return lax.ppermute(value, axes, [(i, i + by) for i in range(peers) if 0 <= i + by < peers])


def gather_pieces(value):
    count = lax.axis_size("tensor")
    pieces = [value] + [None] * (count - 1)
    pieces[1] = swap(value, "tensor", 1)
    for k in range(2, count, 2):
        pieces[k] = swap(value, "tensor", k)
        pieces[k + 1] = swap(pieces[k], "tensor", 1)
    return pieces


def add_low(mine, received):
    return (mine.astype(F32) + received.astype(F32)).astype(BF16)


def scatter_pieces(pieces):
    count = len(pieces)
    evens = [
        add_low(pieces[k], swap(pieces[k + 1], "tensor", 1)) for k in range(0, count, 2)
    ]
    total = evens[0].astype(F32)
    for k in range(2, count, 2):
        total = total + swap(evens[k // 2], "tensor", k).astype(F32)
    return total


def after(value, *deps):
    return lax.optimization_barrier((value,) + deps)[0]


def begin_dp(value, left, bits):
    low = 1 << left.index(bits)
    side = (lax.axis_index("dp") // bits) % 2
    pairs = value.reshape((value.shape[0] // (2 * low), 2, low) + value.shape[1:])
    flat = (value.shape[0] // 2,) + value.shape[1:]
    sent = lax.dynamic_index_in_dim(pairs, 1 - side, 1, keepdims=False).reshape(flat)
    kept = lax.dynamic_index_in_dim(pairs, side, 1, keepdims=False).reshape(flat)
    return kept, swap(sent, "dp", bits), [v for v in left if v != bits]


def finish_dp(state, *deps):
    kept, received, left = state
    received = after(received, *deps) if deps else received
    total = kept.astype(F32) + received.astype(F32)
    return total.astype(BF16), left


def dp_bits():
    return [1 << i for i in range(lax.axis_size("dp").bit_length() - 1)]


def rest_dp(value, left):
    while left:
        value, left = finish_dp(begin_dp(value, left, left[0]))
    return value[0]


def sum_all(value):
    for axis in ("tensor", "dp"):
        bits = 1
        while bits < lax.axis_size(axis):
            value = value + swap(value, axis, bits)
            bits *= 2
    return value


def to_owners_own(value):
    count = lax.axis_size("tensor")
    size = value.shape[1]
    full = jnp.zeros((value.shape[0], count * size), value.dtype)
    return lax.dynamic_update_slice(full, value, (0, lax.axis_index("tensor") * size))


def sum_tensor(value):
    bits = 1
    while bits < lax.axis_size("tensor"):
        value = value + swap(value, "tensor", bits)
        bits *= 2
    return value


def gather_weights(in_weight, out_weight):
    count = lax.axis_size("tensor")
    shape = in_weight.shape[1:]
    low, high = [(lax.axis_index("dp") // b) % 2 == 1 for b in (1, 2)]
    units = [in_weight[0], in_weight[2], in_weight[1], out_weight.reshape(shape)]
    in_pieces = [in_weight, swap(in_weight, "tensor", 1)]
    out_pieces = [out_weight, swap(out_weight, "tensor", 1)]
    for k in range(2, count, 2):
        one = swap(jnp.where(low, units[1], units[0]), "tensor", k)
        two = swap(jnp.where(high, units[3], units[2]), "tensor", k)
        one_other = swap(one, "dp", 1)
        two_other = swap(two, "dp", 2)
        got = [
            jnp.where(low, one_other, one),
            jnp.where(high, two_other, two),
            jnp.where(low, one, one_other),
            jnp.where(high, two, two_other),
        ]
        here = jnp.stack(got)
        there = swap(here, "tensor", 1)
        in_pieces += [here, there]
        out_pieces += [v[3].reshape(out_weight.shape) for v in (here, there)]
    return in_pieces, out_pieces


def to_owners(value):
    count = lax.axis_size("tensor")
    here = lax.axis_index("tensor")
    channels = value.shape[1] // count
    result = jnp.zeros(value.shape, value.dtype)
    for k in range(count):
        block = value[:, k * channels : (k + 1) * channels]
        result = lax.dynamic_update_slice(result, block, (0, (here ^ k) * channels))
    return result


def from_owners(value):
    count = lax.axis_size("tensor")
    here = lax.axis_index("tensor")
    channels = value.shape[1] // count
    return jnp.concatenate(
        [lax.dynamic_slice_in_dim(value, (here ^ k) * channels, channels, 1) for k in range(count)], 1
    )


def matmul(a, b, dims):
    return lax.dot_general(a, b, (dims, ((), ())), preferred_element_type=F32)


ROWS = ((1,), (0,))
BACK = ((1,), (1,))
OUTER = ((0,), (0,))
HEAD = 16
VMEM = 56 << 20


def inverse_rms(values):
    return lax.rsqrt(jnp.mean(values * values, axis=-1, keepdims=True) + EPSILON)


def whole(value):
    return pl.BlockSpec(
        value.shape, lambda *_: (0,) * value.ndim, pipeline_mode=pl.Buffered(1)
    )


def by_rows(block, width):
    return pl.BlockSpec((block, width), lambda i: (i, 0))


def struct(rows, width, kind):
    return jax.ShapeDtypeStruct((rows, width), kind)


def row_block(rows):
    return rows // 3 if rows % 48 == 0 else rows


def params():
    return pltpu.CompilerParams(vmem_limit_bytes=VMEM)


def cost(flops, moved):
    return pl.CostEstimate(flops=flops, bytes_accessed=moved, transcendentals=0)


def mixer_forward_kernel(count, block, *refs):
    x_ref, keep_ref, before_ref, gain_ref, conv_ref = refs[:5]
    in_refs = refs[5 : 5 + count]
    out_refs = refs[5 + count : 5 + 2 * count]
    (
        nin_ref,
        b_ref,
        c_ref,
        v_ref,
        mixed_ref,
        one_ref,
        two_ref,
        gated_ref,
        resid_ref,
        nf_ref,
    ) = refs[5 + 2 * count :]
    start = pl.multiple_of(pl.program_id(0) * block, 16)
    x = x_ref[pl.ds(start, block + HEAD), :].astype(F32)
    nin = (x * inverse_rms(x) * gain_ref[0:1, :]).astype(BF16)
    own = nin[HEAD:]
    nin_ref[...] = own
    keep = keep_ref[...]
    before = before_ref[...]
    resid = x[HEAD:]
    channels = in_refs[0].shape[2]
    for k in range(count):
        cols = slice(k * channels, (k + 1) * channels)
        gate_b = matmul(nin, in_refs[k][0], ROWS)
        value = matmul(nin, in_refs[k][2], ROWS)
        gate_c = matmul(own, in_refs[k][1], ROWS)
        mixed_low = (gate_b * value).astype(BF16)
        mixed = mixed_low.astype(F32)
        one = pltpu.roll(mixed, 1, 0)[HEAD:]
        two = pltpu.roll(mixed, 2, 0)[HEAD:] * before
        conv_out = conv_ref[2:3, cols] * mixed[HEAD:] + keep * (
            conv_ref[1:2, cols] * one + conv_ref[0:1, cols] * two
        )
        gated = (gate_c * conv_out).astype(BF16)
        b_ref[:, cols] = gate_b[HEAD:].astype(BF16)
        c_ref[:, cols] = gate_c.astype(BF16)
        v_ref[:, cols] = value[HEAD:].astype(BF16)
        mixed_ref[:, cols] = mixed_low[HEAD:]
        one_ref[:, cols] = one.astype(BF16)
        two_ref[:, cols] = two.astype(BF16)
        gated_ref[:, cols] = gated
        resid = resid + matmul(gated, out_refs[k][...], ROWS)
    resid_ref[...] = resid
    nf_ref[...] = (resid * inverse_rms(resid) * gain_ref[1:2, :]).astype(BF16)


def mixer_forward(x_ext, keep, before, gains, conv, in_pieces, out_pieces):
    rows, width = keep.shape[0], x_ext.shape[1]
    block = row_block(rows)
    wide = by_rows(block, width)
    narrow = by_rows(block, 1)
    count = len(in_pieces)
    low = struct(rows, width, BF16)
    return pl.pallas_call(
        functools.partial(mixer_forward_kernel, count, block),
        grid=(rows // block,),
        in_specs=[whole(x_ext), narrow, narrow, whole(gains), whole(conv)]
        + [whole(v) for v in in_pieces]
        + [whole(v) for v in out_pieces],
        out_specs=[wide] * 10,
        out_shape=[low] * 8 + [struct(rows, width, F32), low],
        compiler_params=params(),
        cost_estimate=cost(8 * rows * width * width, 30 * rows * width),
        name="mixer_forward",
    )(x_ext, keep, before, gains, conv, *in_pieces, *out_pieces)


def ffn_kernel(pieces, blocks, cuts, *refs):
    nf_a, nf_b, dact_in, up_ref, down_ref = refs[:5]
    nf_out, act_ref, dgate_ref, dup_ref, block_a, block_b, dnf_a, dnf_b = refs[-8:]
    later = pl.program_id(0) >= blocks
    nf = jnp.where(later, nf_b[...], nf_a[...])
    nf_out[...] = nf
    for lo, hi in cuts:
        gate = matmul(nf, up_ref[0, :, lo:hi], ROWS)
        up = matmul(nf, up_ref[1, :, lo:hi], ROWS)
        d_act = dact_in[:, lo:hi].astype(F32)
        sigmoid = 0.5 * jnp.tanh(0.5 * gate) + 0.5
        silu = gate * sigmoid
        act_ref[:, lo:hi] = (silu * up).astype(BF16)
        dup_ref[:, lo:hi] = (d_act * silu).astype(BF16)
        dgate_ref[:, lo:hi] = (d_act * up * (sigmoid + silu * (1.0 - sigmoid))).astype(BF16)
    d_nf = (
        matmul(dgate_ref[...], up_ref[0], BACK) + matmul(dup_ref[...], up_ref[1], BACK)
    ).astype(BF16)
    block = matmul(act_ref[...], down_ref[...], ROWS).astype(BF16)

    @pl.when(later)
    def _():
        block_b[...] = block
        dnf_b[...] = d_nf

    @pl.when(jnp.logical_not(later))
    def _():
        block_a[...] = block
        dnf_a[...] = d_nf


def ffn(nf_a, nf_b, d_act, ffn_weight, down_weight, at, from_block, blocks, held):
    rows, width = nf_a.shape
    hidden = down_weight.shape[0]
    total = d_act.shape[0]
    size = rows // 2
    cuts = [(lo, min(lo + 256, hidden)) for lo in range(0, hidden, 256)]

    def place(i):
        return (at + i // blocks) * 2 + from_block + i % blocks

    def in_a(i):
        return (from_block + jnp.minimum(i, blocks - 1), 0)

    def in_b(i):
        return (from_block + jnp.maximum(i - blocks, 0), 0)

    def out_a(i):
        return (jnp.minimum(i, blocks - 1), 0)

    def out_b(i):
        return (jnp.maximum(i - blocks, 0), 0)

    spot = lambda n: pl.BlockSpec((size, n), lambda i: (place(i), 0))
    operands = [nf_a, nf_b, d_act, ffn_weight, down_weight] + list(held)
    part = struct(blocks * size, width, BF16)
    return pl.pallas_call(
        functools.partial(ffn_kernel, at, blocks, cuts),
        grid=(2 * blocks,),
        in_specs=[
            pl.BlockSpec((size, width), in_a),
            pl.BlockSpec((size, width), in_b),
            spot(hidden),
            whole(ffn_weight),
            whole(down_weight),
        ]
        + [pl.BlockSpec(memory_space=pl.ANY)] * len(held),
        out_specs=[spot(width), spot(hidden), spot(hidden), spot(hidden)]
        + [pl.BlockSpec((size, width), m) for m in (out_a, out_b, out_a, out_b)],
        out_shape=[struct(total, width, BF16)] + [struct(total, hidden, BF16)] * 3 + [part] * 4,
        input_output_aliases={5 + i: i for i in range(len(held))},
        compiler_params=params(),
        cost_estimate=cost(20 * blocks * size * width * hidden, 40 * blocks * size * width),
        name="ffn",
    )(*operands)


def first_step():
    return pl.program_id(0) == 0


def add_rows(ref, at, cols, value):
    ref[at : at + 1, cols] += jnp.sum(value, axis=0, keepdims=True)


def mixer_middle_kernel(count, *refs):
    dnf_ref, g_ref, resid_ref, gain_ref, conv_ref, keep_ref = refs[:6]
    c_ref, mixed_ref, one_ref, two_ref = refs[6:10]
    out_refs = refs[10 : 10 + count]
    dres_ref, low_ref, dcgate_ref, dconv_ref, sums_ref = refs[10 + count :]

    @pl.when(first_step())
    def _():
        sums_ref[...] = jnp.zeros_like(sums_ref)

    d_nf = dnf_ref[...].astype(F32)
    resid = resid_ref[...]
    inverse = inverse_rms(resid)
    normed = resid * inverse
    scaled = d_nf * gain_ref[1:2, :]
    d_res = g_ref[...].astype(F32) + inverse * (
        scaled - normed * jnp.mean(scaled * normed, axis=-1, keepdims=True)
    )
    low = d_res.astype(BF16)
    dres_ref[...] = d_res
    low_ref[...] = low
    add_rows(sums_ref, 3, slice(None), d_nf * normed)
    keep = keep_ref[...]
    channels = out_refs[0].shape[0]
    for k in range(count):
        cols = slice(k * channels, (k + 1) * channels)
        d_gated = matmul(low, out_refs[k][...], BACK)
        mixed = mixed_ref[:, cols].astype(F32)
        one = one_ref[:, cols].astype(F32)
        two = two_ref[:, cols].astype(F32)
        conv_out = conv_ref[2:3, cols] * mixed + keep * (
            conv_ref[1:2, cols] * one + conv_ref[0:1, cols] * two
        )
        dcgate_ref[:, cols] = (d_gated * conv_out).astype(BF16)
        d_conv = d_gated * c_ref[:, cols].astype(F32)
        dconv_ref[:, cols] = d_conv
        weighted = keep * d_conv
        add_rows(sums_ref, 0, cols, weighted * two)
        add_rows(sums_ref, 1, cols, weighted * one)
        add_rows(sums_ref, 2, cols, d_conv * mixed)


def mixer_middle(d_nf, g, resid, gains, conv, keep, gate_c, mixed, one, two, out_pieces):
    rows, width = resid.shape
    block = row_block(rows)
    wide = by_rows(block, width)
    count = len(out_pieces)
    return pl.pallas_call(
        functools.partial(mixer_middle_kernel, count),
        grid=(rows // block,),
        in_specs=[wide] * 3 + [whole(gains), whole(conv), by_rows(block, 1)] + [wide] * 4
        + [whole(v) for v in out_pieces],
        out_specs=[wide] * 4 + [pl.BlockSpec((8, width), lambda i: (0, 0))],
        out_shape=[
            struct(rows, width, F32),
            struct(rows, width, BF16),
            struct(rows, width, BF16),
            struct(rows, width, F32),
            struct(8, width, F32),
        ],
        compiler_params=params(),
        cost_estimate=cost(2 * rows * width * width, 30 * rows * width),
        name="mixer_middle",
    )(d_nf, g, resid, gains, conv, keep, gate_c, mixed, one, two, *out_pieces)


def mixer_last_kernel(count, steps, *refs):
    dconv_ref, next_ref, after_ref, keep_ref, keep_next_ref, keep_after_ref = refs[:6]
    b_ref, v_ref, dcgate_ref, x_ref, dres_ref, gain_ref, conv_ref = refs[6:13]
    in_refs = refs[13 : 13 + count]
    db_ref, dv_ref, grad_ref, sums_ref = refs[13 + count :]

    @pl.when(first_step())
    def _():
        sums_ref[...] = jnp.zeros_like(sums_ref)

    last = pl.program_id(0) == steps - 1
    keep = keep_ref[...]
    keep_after = keep_after_ref[...]
    rows = keep.shape[0]
    channels = in_refs[0].shape[2]
    d_ni = None
    for k in range(count):
        cols = slice(k * channels, (k + 1) * channels)
        d_conv = dconv_ref[:, cols]
        following = jnp.where(
            last, after_ref[:, cols], keep_next_ref[...] * next_ref[:, cols]
        )
        ahead = jnp.concatenate([keep * d_conv, following], 0)
        size = rows + 8
        d_mixed = (
            conv_ref[2:3, cols] * d_conv
            + conv_ref[1:2, cols] * pltpu.roll(ahead, size - 1, 0)[:rows]
            + conv_ref[0:1, cols] * keep_after * pltpu.roll(ahead, size - 2, 0)[:rows]
        )
        d_b = (d_mixed * v_ref[:, cols].astype(F32)).astype(BF16)
        d_v = (d_mixed * b_ref[:, cols].astype(F32)).astype(BF16)
        db_ref[:, cols] = d_b
        dv_ref[:, cols] = d_v
        part = (
            matmul(d_b, in_refs[k][0], BACK)
            + matmul(dcgate_ref[:, cols], in_refs[k][1], BACK)
            + matmul(d_v, in_refs[k][2], BACK)
        )
        d_ni = part if d_ni is None else d_ni + part
    x = x_ref[...].astype(F32)
    inverse = inverse_rms(x)
    normed = x * inverse
    scaled = d_ni * gain_ref[0:1, :]
    grad_ref[...] = dres_ref[...] + inverse * (
        scaled - normed * jnp.mean(scaled * normed, axis=-1, keepdims=True)
    )
    add_rows(sums_ref, 0, slice(None), d_ni * normed)


def mixer_last(
    d_conv, after, keep, keep_after, gate_b, value, d_cgate, x, d_res, gains, conv, in_pieces
):
    rows, width = d_conv.shape
    block = row_block(rows)
    steps = rows // block
    wide = by_rows(block, width)
    narrow = by_rows(block, 1)
    count = len(in_pieces)
    ahead = lambda i: (jnp.minimum((i + 1) * (block // 8), rows // 8 - 1), 0)
    return pl.pallas_call(
        functools.partial(mixer_last_kernel, count, steps),
        grid=(steps,),
        in_specs=[
            wide,
            pl.BlockSpec((8, width), ahead),
            whole(after),
            narrow,
            pl.BlockSpec((8, 1), ahead),
            narrow,
        ]
        + [wide] * 5
        + [whole(gains), whole(conv)]
        + [whole(v) for v in in_pieces],
        out_specs=[wide] * 3 + [pl.BlockSpec((8, width), lambda i: (0, 0))],
        out_shape=[
            struct(rows, width, BF16),
            struct(rows, width, BF16),
            struct(rows, width, F32),
            struct(8, width, F32),
        ],
        compiler_params=params(),
        cost_estimate=cost(6 * rows * width * width, 30 * rows * width),
        name="mixer_last",
    )(
        d_conv, d_conv, after, keep, keep, keep_after,
        gate_b, value, d_cgate, x, d_res, gains, conv, *in_pieces,
    )


def body(
    tokens,
    starts,
    norm_gains,
    in_weight,
    conv_weight,
    out_weight,
    ffn_weight,
    down_weight,
    cotangent,
):
    row_count, width = tokens.shape
    count = lax.axis_size("tensor")
    dp_count = lax.axis_size("dp")
    here = lax.axis_index("tensor")
    rows = row_count // count
    first = here * rows

    keep_all = 1.0 - starts.astype(F32)
    edge = jnp.concatenate(
        [tokens[-HEAD:], jnp.broadcast_to(keep_all[-1], (HEAD, width)).astype(BF16)], 0
    )
    before = shift(edge, "dp", 1)
    back = jnp.maximum(first - HEAD, 0)
    head_rows = jnp.where(
        here == 0, before[:HEAD], lax.dynamic_slice_in_dim(tokens, back, HEAD, 0)
    )
    keep_prev = jnp.where(
        here == 0,
        before[HEAD, 0].astype(F32),
        lax.dynamic_index_in_dim(keep_all, jnp.maximum(first - 1, 0), 0, False),
    )
    keep = lax.dynamic_slice_in_dim(keep_all, first, rows, 0)
    keep_before = jnp.concatenate([keep_prev[None], keep[:-1]])[:, None]
    keep_after = jnp.concatenate([keep[1:], jnp.ones((1,), F32)])[:, None]
    keep = keep[:, None]

    in_pieces, out_pieces = gather_weights(in_weight, out_weight)
    conv = from_owners(sum_tensor(to_owners_own(conv_weight)))
    x_share = lax.dynamic_slice_in_dim(tokens, first, rows, 0)
    x_ext = jnp.concatenate([head_rows, x_share], 0)
    g_all = jnp.concatenate(
        [lax.dynamic_slice_in_dim(cotangent, (here ^ k) * rows, rows, 0) for k in range(count)], 0
    )

    d_act = matmul(g_all, down_weight, BACK).astype(BF16)
    x_ext = after(x_ext, d_act)

    normed_in, gate_b, gate_c, value, mixed, one, two, gated_mix, resid, normed_ffn = mixer_forward(
        x_ext, keep, keep_before, norm_gains, conv, in_pieces, out_pieces
    )

    near = swap(normed_ffn, "tensor", 1)
    far = {k: swap(normed_ffn, "tensor", k) for k in range(2, count, 2)}
    *held, block_a, block_b, dnf_a, dnf_b = ffn(
        normed_ffn, near, d_act, ffn_weight, down_weight, 0, 0, 2, ()
    )
    dnf_own = add_low(dnf_a, swap(dnf_b, "tensor", 1))
    block_own = add_low(block_a, swap(block_b, "tensor", 1))
    dnf_far = {}
    block_far = {}
    for k in range(2, count, 2):
        nf_a = after(far[k], block_a)
        *held, block_a, block_b, dnf_a, dnf_b = ffn(
            nf_a, swap(nf_a, "tensor", 1), d_act, ffn_weight, down_weight, k, 0, 2, held
        )
        dnf_far[k] = swap(add_low(dnf_a, swap(dnf_b, "tensor", 1)), "tensor", k)
        block_far[k] = (block_a, swap(block_b, "tensor", 1))
    nf_all, act, d_gate, d_up = held
    split = (dp_count, width // dp_count, -1)
    bits = dp_bits()
    grad_down = matmul(g_all, act, OUTER).astype(BF16)
    down = begin_dp(grad_down.reshape(split), bits, 1)
    grad_gate = matmul(nf_all, after(d_gate, grad_down), OUTER).astype(BF16)
    gate = begin_dp(grad_gate.reshape(split), bits, 2)
    grad_up = matmul(nf_all, after(d_up, grad_gate), OUTER).astype(BF16)
    up = begin_dp(grad_up.reshape(split), bits, 1)
    down = begin_dp(*finish_dp(down, grad_up), 2)
    block_sum = block_own.astype(F32)
    for k in range(2, count, 2):
        part = add_low(*block_far[k])
        block_sum = block_sum + swap(after(part, dnf_far[k]), "tensor", k).astype(F32)

    d_nf = dnf_own.astype(F32)
    for k in range(2, count, 2):
        d_nf = d_nf + after(dnf_far[k], down[0]).astype(F32)
    g_share = g_all[:rows]
    d_res, d_res_low, d_cgate, d_conv, sums = mixer_middle(
        d_nf, g_share, resid, norm_gains, conv, keep, gate_c, mixed, one, two, out_pieces
    )
    edge_back = jnp.stack([keep[0] * d_conv[0], keep[0] * (keep[1] * d_conv[1])])
    back_edge = shift(to_owners(edge_back), ("dp", "tensor"), -1)
    gate = begin_dp(*finish_dp(gate, d_conv), 1)
    grad_out = matmul(d_res_low, gated_mix, OUTER).astype(BF16)
    grad_c = matmul(normed_in, d_cgate, OUTER).astype(BF16)

    channels = width // count

    def core_scatter(grads, *deps):
        def side(parity):
            blocks = [
                jnp.stack(
                    [
                        g[:, k * channels : (k + 1) * channels].reshape(
                            dp_count, width // dp_count, channels
                        )
                        for k in range(parity, count, 2)
                    ],
                    1,
                )
                for g in grads
            ]
            return jnp.stack(blocks, 1)

        return side(0), swap(side(1), "tensor", 1)

    def y_scatter(value):
        total = value[:, :, 0].astype(F32)
        for k in range(2, count, 2):
            total = total + swap(value[:, :, k // 2], "tensor", k).astype(F32)
        return total

    first_group = core_scatter([grad_c, grad_out])
    received = from_owners(after(back_edge, grad_c))
    received = jnp.concatenate([received, jnp.zeros((6, width), F32)], 0)
    d_b, d_v, grad_tokens, gain_one = mixer_last(
        d_conv, received, keep, keep_after, gate_b, value, d_cgate, x_share, d_res,
        norm_gains, conv, in_pieces,
    )
    up = begin_dp(*finish_dp(up, d_b), 2)
    first_group = add_low(after(first_group[0], d_b), first_group[1])
    first_group = y_scatter(first_group).astype(BF16)
    grad_b = matmul(normed_in, d_b, OUTER).astype(BF16)
    grad_v = matmul(normed_in, d_v, OUTER).astype(BF16)
    second_group = add_low(*core_scatter([grad_b, grad_v]))
    down = begin_dp(*finish_dp(down, grad_v), bits[2])
    gate = begin_dp(*finish_dp(gate, grad_v), bits[2])
    second = begin_dp(second_group, bits, 1)
    up = begin_dp(*finish_dp(up, second[0]), bits[2])
    first_group = rest_dp(first_group, bits)
    second_group = y_scatter(rest_dp(*finish_dp(second))[None])[0]
    out_down, out_gate, out_up = [
        rest_dp(*finish_dp(v)).astype(F32) for v in (down, gate, up)
    ]
    out_c, out_o = first_group.astype(F32)
    out_b, out_v = second_group
    block_out = (resid + block_sum).astype(BF16)
    small = sum_all(jnp.concatenate([gain_one[:1], sums[3:4], to_owners(sums[:3])], 0))
    return (
        block_out,
        grad_tokens,
        small[:2],
        jnp.stack([out_b, out_c, out_v]),
        small[2:],
        out_o.T,
        jnp.stack([out_gate, out_up]),
        out_down.T,
    )


def solution(mesh):
    return jax.shard_map(
        body,
        mesh=mesh,
        in_specs=(
            P("dp", None),
            P("dp"),
            P(),
            P(None, None, "tensor"),
            P(None, "tensor"),
            P("tensor", None),
            P(None, None, "tensor"),
            P("tensor", None),
            P("dp", None),
        ),
        out_specs=(
            P(("dp", "tensor"), None),
            P(("dp", "tensor"), None),
            P(),
            P(None, "dp", "tensor"),
            P(),
            P("tensor", "dp"),
            P(None, "dp", "tensor"),
            P("tensor", "dp"),
        ),
        check_vma=False,
    )
```

```python
import functools

import jax
import jax.numpy as jnp
from jax import lax
from jax.experimental import pallas as pl
from jax.experimental.pallas import tpu as pltpu
from jax.sharding import PartitionSpec as P

EPSILON = 1e-05
F32 = jnp.float32
BF16 = jnp.bfloat16


def swap(value, axis, bits):
    peers = lax.axis_size(axis)
    return lax.ppermute(value, axis, [(i, i ^ bits) for i in range(peers)])


def shift(value, axes, by):
    peers = lax.axis_size(axes)
    return lax.ppermute(value, axes, [(i, i + by) for i in range(peers) if 0 <= i + by < peers])


def gather_pieces(value):
    count = lax.axis_size("tensor")
    pieces = [value] + [None] * (count - 1)
    pieces[1] = swap(value, "tensor", 1)
    for k in range(2, count, 2):
        pieces[k] = swap(value, "tensor", k)
        pieces[k + 1] = swap(pieces[k], "tensor", 1)
    return pieces


def after(value, *deps):
    return lax.optimization_barrier((value,) + deps)[0]


def dp_bits():
    return [1 << i for i in range(lax.axis_size("dp").bit_length() - 1)]


def gather_far(packed, k, ready, later):
    low = lax.axis_index("dp") % 2
    one = swap(jnp.where(low == 1, packed[2], packed[0]), "tensor", k)
    rest = swap(packed[1::2], "tensor", k)
    one = after(one, ready)
    other = after(swap(one, "dp", 1), later)
    rest = after(rest, later)
    far = jnp.stack(
        [
            jnp.where(low == 0, one, other),
            rest[0],
            jnp.where(low == 0, other, one),
            rest[1],
        ]
    )
    return [far, swap(far, "tensor", 1)]


def to_owners(value):
    count = lax.axis_size("tensor")
    here = lax.axis_index("tensor")
    channels = value.shape[1] // count
    result = jnp.zeros(value.shape, value.dtype)
    for k in range(count):
        block = value[:, k * channels : (k + 1) * channels]
        result = lax.dynamic_update_slice(result, block, (0, (here ^ k) * channels))
    return result


def matmul(a, b, dims):
    return lax.dot_general(a, b, (dims, ((), ())), preferred_element_type=F32)


ROWS = ((1,), (0,))
BACK = ((1,), (1,))
OUTER = ((0,), (0,))
HEAD = 16
VMEM = 56 << 20


def inverse_rms(values):
    return lax.rsqrt(jnp.mean(values * values, axis=-1, keepdims=True) + EPSILON)


def whole(value):
    return pl.BlockSpec(
        value.shape, lambda *_: (0,) * len(value.shape), pipeline_mode=pl.Buffered(1)
    )


def units(value, first, count):
    return pl.BlockSpec(
        (count,) + value.shape[1:], lambda *_: (first, 0, 0), pipeline_mode=pl.Buffered(1)
    )


def by_rows(block, width):
    return pl.BlockSpec((block, width), lambda i: (i, 0))


def struct(rows, width, kind):
    return jax.ShapeDtypeStruct((rows, width), kind)


def row_block(rows):
    return rows // 3 if rows % 48 == 0 else rows


def params():
    return pltpu.CompilerParams(vmem_limit_bytes=VMEM)


def cost():
    return pl.CostEstimate(flops=1, bytes_accessed=1, transcendentals=0)


def fold_kernel(low_from, low_to, side_ref, kept_ref, *refs):
    outs = refs[-1:] if low_to is None else refs[-2:]
    received = refs[: len(refs) - len(outs)]
    count = received[0].shape[0]

    def total(i):
        at = i
        if low_from is not None:
            at = (i // low_from) * (2 * low_from) + i % low_from + side_ref[0] * low_from
        value = kept_ref[at].astype(F32)
        for ref in received:
            value = value + ref[i].astype(F32)
        return value.astype(outs[0].dtype)

    if low_to is None:
        for i in range(count):
            outs[0][i] = total(i)
    else:
        for j in range(count // 2):
            base = (j // low_to) * (2 * low_to) + j % low_to
            outs[0][j] = total(base + (1 - side_ref[1]) * low_to)
            outs[1][j] = total(base + side_ref[1] * low_to)


def fold(kept, received, low_from=None, from_bits=1, low_to=None, to_bits=1, kind=BF16):
    count, rows, width = received[0].shape
    steps = 2 if rows % 32 == 0 and count * rows * width > 700000 else 1
    block = rows // steps
    place = lax.axis_index("dp")
    sides = jnp.stack([(place // from_bits) % 2, (place // to_bits) % 2]).astype(jnp.int32)
    spec = lambda n: pl.BlockSpec((n, block, width), lambda i: (0, i, 0))
    outs = [count] if low_to is None else [count // 2] * 2
    result = pl.pallas_call(
        functools.partial(fold_kernel, low_from, low_to),
        grid=(rows // block,),
        in_specs=[pl.BlockSpec(memory_space=pltpu.SMEM), spec(kept.shape[0])]
        + [spec(count)] * len(received),
        out_specs=[spec(n) for n in outs],
        out_shape=[jax.ShapeDtypeStruct((n, rows, width), kind) for n in outs],
        compiler_params=params(),
        cost_estimate=cost(),
        name="fold",
    )(sides, kept, *received)
    return result[0] if low_to is None else result


def add_low(mine, received):
    return fold(mine[None], [received[None]])[0]


def step(state, bits, *deps):
    kept, source, received, left = state
    received = after(received, *deps) if deps else received
    low = 1 << left.index(bits)
    source = {} if source is None else dict(low_from=source[0], from_bits=source[1])
    sent, kept = fold(kept, [received], low_to=low, to_bits=bits, **source)
    return kept, None, swap(sent, "dp", bits), [v for v in left if v != bits]


def close(state, *deps):
    kept, source, received, left = state
    while left:
        state = step(state, left[0], *deps)
        kept, source, received, left = state
    received = after(received, *deps) if deps else received
    return kept.astype(F32) + received.astype(F32)


def mixer_grad_kernel(count, places, lefts_count, *refs):
    lefts, rights = refs[:lefts_count], refs[lefts_count:-2]
    even_ref, odd_ref = refs[-2:]
    channels = even_ref.shape[4]
    rows = even_ref.shape[3]
    for m, right in enumerate(rights):
        left = lefts[min(m, len(lefts) - 1)][...]
        for k in range(count):
            ref = odd_ref if k % 2 else even_ref
            part = matmul(left, right[:, k * channels : (k + 1) * channels], OUTER)
            ref[:, m, k // 2] = part.astype(BF16).reshape(places, rows, channels)


def mixer_grad(lefts, rights, count):
    width = lefts[0].shape[1]
    places = lax.axis_size("dp")
    shape = jax.ShapeDtypeStruct(
        (places, len(rights), count // 2, width // places, rights[0].shape[1] // count), BF16
    )
    operands = list(lefts) + list(rights)
    return pl.pallas_call(
        functools.partial(mixer_grad_kernel, count, places, len(lefts)),
        grid=(1,),
        in_specs=[whole(v) for v in operands],
        out_specs=[whole(shape)] * 2,
        out_shape=[shape] * 2,
        compiler_params=params(),
        cost_estimate=cost(),
        name="mixer_grad",
    )(*operands)


def chip_sums_kernel(mine_ref, received_ref, *outs):
    for j, out in enumerate(outs):
        total = mine_ref[:, :, j].astype(F32) + received_ref[:, :, j].astype(F32)
        out[...] = total.astype(BF16)


def chip_sums(mine, received):
    places, kinds, chips, rows, channels = mine.shape
    out = jax.ShapeDtypeStruct((places, kinds, rows, channels), BF16)
    return pl.pallas_call(
        chip_sums_kernel,
        grid=(2,),
        in_specs=[pl.BlockSpec((places // 2,) + mine.shape[1:], lambda i: (i, 0, 0, 0, 0))] * 2,
        out_specs=[pl.BlockSpec((places // 2,) + out.shape[1:], lambda i: (i, 0, 0, 0))] * chips,
        out_shape=[out] * chips,
        compiler_params=params(),
        cost_estimate=cost(),
        name="chip_sums",
    )(mine, received)


def mixer_forward_kernel(count, block, is_first, is_last, *refs):
    x_ref, keep_ref, before_ref, gain_ref, conv_ref = refs[:5]
    weights = refs[5 : 5 + count]
    rest = list(refs[5 + count :])
    start = pl.multiple_of(pl.program_id(0) * block, 16)
    x = x_ref[pl.ds(start, block + HEAD), :].astype(F32)
    nin = (x * inverse_rms(x) * gain_ref[0:1, :]).astype(BF16)
    own = nin[HEAD:]
    keep = keep_ref[...]
    before = before_ref[...]
    resid = x[HEAD:] if is_first else rest.pop(0)[...]
    b_ref, c_ref, v_ref, mixed_ref, one_ref, two_ref, gated_ref, resid_ref = rest[:8]
    if is_first:
        rest[8][...] = own
    channels = weights[0].shape[2]
    for k in range(count):
        cols = slice(k * channels, (k + 1) * channels)
        gate_b = matmul(nin, weights[k][0], ROWS)
        value = matmul(nin, weights[k][2], ROWS)
        gate_c = matmul(own, weights[k][1], ROWS)
        mixed_low = (gate_b * value).astype(BF16)
        mixed = mixed_low.astype(F32)
        one = pltpu.roll(mixed, 1, 0)[HEAD:]
        two = pltpu.roll(mixed, 2, 0)[HEAD:] * before
        conv_out = conv_ref[2:3, cols] * mixed[HEAD:] + keep * (
            conv_ref[1:2, cols] * one + conv_ref[0:1, cols] * two
        )
        gated = (gate_c * conv_out).astype(BF16)
        b_ref[:, cols] = gate_b[HEAD:].astype(BF16)
        c_ref[:, cols] = gate_c.astype(BF16)
        v_ref[:, cols] = value[HEAD:].astype(BF16)
        mixed_ref[:, cols] = mixed_low[HEAD:]
        one_ref[:, cols] = one.astype(BF16)
        two_ref[:, cols] = two.astype(BF16)
        gated_ref[:, cols] = gated
        resid = resid + matmul(gated, weights[k][3], BACK)
    resid_ref[...] = resid
    if is_last:
        rest[-1][...] = (resid * inverse_rms(resid) * gain_ref[1:2, :]).astype(BF16)


def mixer_forward(x_ext, keep, before, gains, conv, pieces, resid, is_last):
    rows, width = keep.shape[0], x_ext.shape[1]
    block = row_block(rows)
    wide = by_rows(block, width)
    narrow = by_rows(block, 1)
    count = len(pieces)
    is_first = resid is None
    channels = count * pieces[0].shape[2]
    shapes = [struct(rows, channels, BF16)] * 7 + [struct(rows, width, F32)]
    shapes += [struct(rows, width, BF16)] * (is_first + is_last)
    carried = [] if is_first else [resid]
    return pl.pallas_call(
        functools.partial(mixer_forward_kernel, count, block, is_first, is_last),
        grid=(rows // block,),
        in_specs=[whole(x_ext), narrow, narrow, whole(gains), whole(conv)]
        + [whole(v) for v in pieces]
        + [wide] * len(carried),
        out_specs=[by_rows(block, v.shape[1]) for v in shapes],
        out_shape=shapes,
        compiler_params=params(),
        cost_estimate=cost(),
        name="mixer_forward",
    )(x_ext, keep, before, gains, conv, *pieces, *carried)


def act_grad_kernel(place_ref, g_ref, down_ref, g_out, d_act_ref):
    g = g_ref[...]
    g_out[...] = g
    d_act_ref[...] = matmul(g, down_ref[...], BACK).astype(BF16)


def act_grad(here, count, cotangent, down_weight):
    total, width = cotangent.shape
    hidden = down_weight.shape[0]
    size = total // (2 * count)
    spot = lambda n: pl.BlockSpec((size, n), lambda i, place: (i, 0))
    return pl.pallas_call(
        act_grad_kernel,
        grid_spec=pltpu.PrefetchScalarGridSpec(
            num_scalar_prefetch=1,
            grid=(2 * count,),
            in_specs=[
                pl.BlockSpec((size, width), lambda i, place: ((place[0] ^ (i // 2)) * 2 + i % 2, 0)),
                whole(down_weight),
            ],
            out_specs=[spot(width), spot(hidden)],
        ),
        out_shape=[struct(total, width, BF16), struct(total, hidden, BF16)],
        compiler_params=params(),
        cost_estimate=cost(),
        name="act_grad",
    )(here.astype(jnp.int32)[None], cotangent, down_weight)


def ffn_kernel(pieces, blocks, cuts, *refs):
    nf_a, nf_b, dact_in, up_ref, down_ref = refs[:5]
    nf_out, act_ref, dgu_ref, block_a, block_b, dnf_a, dnf_b = refs[-7:]
    later = pl.program_id(0) >= blocks
    nf = jnp.where(later, nf_b[...], nf_a[...])
    nf_out[...] = nf
    for lo, hi in cuts:
        gate = matmul(nf, up_ref[0, :, lo:hi], ROWS)
        up = matmul(nf, up_ref[1, :, lo:hi], ROWS)
        d_act = dact_in[:, lo:hi].astype(F32)
        sigmoid = 0.5 * jnp.tanh(0.5 * gate) + 0.5
        silu = gate * sigmoid
        act_ref[:, lo:hi] = (silu * up).astype(BF16)
        dgu_ref[1, :, lo:hi] = (d_act * silu).astype(BF16)
        dgu_ref[0, :, lo:hi] = (d_act * up * (sigmoid + silu * (1.0 - sigmoid))).astype(BF16)
    d_nf = (
        matmul(dgu_ref[0], up_ref[0], BACK) + matmul(dgu_ref[1], up_ref[1], BACK)
    ).astype(BF16)
    block = matmul(act_ref[...], down_ref[...], ROWS).astype(BF16)

    @pl.when(later)
    def _():
        block_b[...] = block
        dnf_b[...] = d_nf

    @pl.when(jnp.logical_not(later))
    def _():
        block_a[...] = block
        dnf_a[...] = d_nf


def ffn(nf_a, nf_b, d_act, ffn_weight, down_weight, at, from_block, blocks, held):
    rows, width = nf_a.shape
    hidden = down_weight.shape[0]
    total = d_act.shape[0]
    size = rows // 2
    cuts = [(lo, min(lo + 256, hidden)) for lo in range(0, hidden, 256)]

    def place(i):
        return (at + i // blocks) * 2 + from_block + i % blocks

    def in_a(i):
        return (from_block + jnp.minimum(i, blocks - 1), 0)

    def in_b(i):
        return (from_block + jnp.maximum(i - blocks, 0), 0)

    def out_a(i):
        return (jnp.minimum(i, blocks - 1), 0)

    def out_b(i):
        return (jnp.maximum(i - blocks, 0), 0)

    spot = lambda n: pl.BlockSpec((size, n), lambda i: (place(i), 0))
    operands = [nf_a, nf_b, d_act, ffn_weight, down_weight] + list(held)
    part = struct(blocks * size, width, BF16)
    return pl.pallas_call(
        functools.partial(ffn_kernel, at, blocks, cuts),
        grid=(2 * blocks,),
        in_specs=[
            pl.BlockSpec((size, width), in_a),
            pl.BlockSpec((size, width), in_b),
            spot(hidden),
            whole(ffn_weight),
            whole(down_weight),
        ]
        + [pl.BlockSpec(memory_space=pl.ANY)] * len(held),
        out_specs=[
            spot(width),
            spot(hidden),
            pl.BlockSpec((2, size, hidden), lambda i: (0, place(i), 0)),
        ]
        + [pl.BlockSpec((size, width), m) for m in (out_a, out_b, out_a, out_b)],
        out_shape=[
            struct(total, width, BF16),
            struct(total, hidden, BF16),
            jax.ShapeDtypeStruct((2, total, hidden), BF16),
        ]
        + [part] * 4,
        input_output_aliases={5 + i: i for i in range(len(held))},
        compiler_params=params(),
        cost_estimate=cost(),
        name="ffn",
    )(*operands)


def first_step():
    return pl.program_id(0) == 0


def add_rows(ref, at, cols, value):
    ref[at : at + 1, cols] += jnp.sum(value, axis=0, keepdims=True)


def pick(refs, k, channels):
    at = (k % 2) * channels
    return refs[k // 2][:, at : at + channels].astype(F32)


def mixer_middle_kernel(count, *refs):
    parts = count // 2
    g_ref, resid_ref, gain_ref, conv_ref, keep_ref = refs[:5]
    dnf_refs, c_refs, mixed_refs, one_refs, two_refs = [
        refs[5 + i * parts : 5 + (i + 1) * parts] for i in range(5)
    ]
    refs = refs[5 + 5 * parts :]
    weights = refs[:count]
    dres_ref, low_ref, dcgate_ref, dconv_ref, sums_ref, edge_ref = refs[count:]
    is_first = first_step()

    @pl.when(first_step())
    def _():
        sums_ref[...] = jnp.zeros_like(sums_ref)

    d_nf = dnf_refs[0][...].astype(F32)
    for ref in dnf_refs[1:]:
        d_nf = d_nf + ref[...].astype(F32)
    resid = resid_ref[...]
    inverse = inverse_rms(resid)
    normed = resid * inverse
    scaled = d_nf * gain_ref[1:2, :]
    d_res = g_ref[...].astype(F32) + inverse * (
        scaled - normed * jnp.mean(scaled * normed, axis=-1, keepdims=True)
    )
    low = d_res.astype(BF16)
    dres_ref[...] = d_res
    low_ref[...] = low
    add_rows(sums_ref, 3, slice(None), d_nf * normed)
    keep = keep_ref[...]
    channels = weights[0].shape[2]
    for k in range(count):
        cols = slice(k * channels, (k + 1) * channels)
        d_gated = matmul(low, weights[k][0], ROWS)
        mixed, one, two = [pick(v, k, channels) for v in (mixed_refs, one_refs, two_refs)]
        conv_out = conv_ref[2:3, cols] * mixed + keep * (
            conv_ref[1:2, cols] * one + conv_ref[0:1, cols] * two
        )
        dcgate_ref[:, cols] = (d_gated * conv_out).astype(BF16)
        d_conv = d_gated * pick(c_refs, k, channels)
        dconv_ref[:, cols] = d_conv.astype(BF16)
        weighted = keep * d_conv

        @pl.when(is_first)
        def _():
            row = lax.broadcasted_iota(jnp.int32, (8, channels), 0)
            edge = keep[:8] * d_conv[:8]
            edge_ref[k] = jnp.where(row == 1, keep[0:1] * edge, edge)

        add_rows(sums_ref, 0, cols, weighted * two)
        add_rows(sums_ref, 1, cols, weighted * one)
        add_rows(sums_ref, 2, cols, d_conv * mixed)


def mixer_middle(g, resid, gains, conv, keep, d_nf, gate_c, mixed, one, two, pieces):
    rows, width = resid.shape
    block = row_block(rows)
    wide = by_rows(block, width)
    count = len(pieces)
    many = d_nf + gate_c + mixed + one + two
    return pl.pallas_call(
        functools.partial(mixer_middle_kernel, count),
        grid=(rows // block,),
        in_specs=[wide] * 2
        + [whole(gains), whole(conv), by_rows(block, 1)]
        + [by_rows(block, v.shape[1]) for v in many]
        + [units(v, 3, 1) for v in pieces],
        out_specs=[wide] * 4
        + [
            pl.BlockSpec((8, width), lambda i: (0, 0)),
            pl.BlockSpec((count, 8, width // count), lambda i: (0, 0, 0)),
        ],
        out_shape=[
            struct(rows, width, F32),
            struct(rows, width, BF16),
            struct(rows, width, BF16),
            struct(rows, width, BF16),
            struct(8, width, F32),
            jax.ShapeDtypeStruct((count, 8, width // count), F32),
        ],
        compiler_params=params(),
        cost_estimate=cost(),
        name="mixer_middle",
    )(g, resid, gains, conv, keep, *many, *pieces)


def mixer_last_kernel(count, steps, *refs):
    mask_ref, refs = refs[0], refs[1:]
    dconv_ref, next_ref, after_ref, keep_ref, keep_next_ref, keep_after_ref = refs[:6]
    dcgate_ref, x_ref, dres_ref, gain_ref, conv_ref = refs[6:11]
    parts = count // 2
    b_refs = refs[11 : 11 + parts]
    v_refs = refs[11 + parts : 11 + count]
    weights = refs[11 + count : 11 + 2 * count]
    db_ref, dv_ref, grad_ref, sums_ref = refs[11 + 2 * count :]

    @pl.when(first_step())
    def _():
        sums_ref[...] = jnp.zeros_like(sums_ref)

    last = pl.program_id(0) == steps - 1
    keep = keep_ref[...]
    keep_after = keep_after_ref[...]
    rows = keep.shape[0]
    channels = weights[0].shape[2]
    d_ni = None
    for k in range(count):
        cols = slice(k * channels, (k + 1) * channels)
        d_conv = dconv_ref[:, cols].astype(F32)
        beyond = after_ref[k ^ mask_ref[0]]
        beyond = jnp.concatenate([beyond, jnp.zeros_like(beyond)], 0)
        following = jnp.where(
            last, beyond, keep_next_ref[...] * next_ref[:, cols].astype(F32)
        )
        ahead = jnp.concatenate([keep * d_conv, following], 0)
        size = rows + 16
        d_mixed = (
            conv_ref[2:3, cols] * d_conv
            + conv_ref[1:2, cols] * pltpu.roll(ahead, size - 1, 0)[:rows]
            + conv_ref[0:1, cols] * keep_after * pltpu.roll(ahead, size - 2, 0)[:rows]
        )
        d_b = (d_mixed * pick(v_refs, k, channels)).astype(BF16)
        d_v = (d_mixed * pick(b_refs, k, channels)).astype(BF16)
        db_ref[:, cols] = d_b
        dv_ref[:, cols] = d_v
        part = (
            matmul(d_b, weights[k][0], BACK)
            + matmul(dcgate_ref[:, cols], weights[k][1], BACK)
            + matmul(d_v, weights[k][2], BACK)
        )
        d_ni = part if d_ni is None else d_ni + part
    x = x_ref[...].astype(F32)
    inverse = inverse_rms(x)
    normed = x * inverse
    scaled = d_ni * gain_ref[0:1, :]
    grad_ref[...] = dres_ref[...] + inverse * (
        scaled - normed * jnp.mean(scaled * normed, axis=-1, keepdims=True)
    )
    add_rows(sums_ref, 0, slice(None), d_ni * normed)


def mixer_last(
    mask, d_conv, after, keep, keep_after, gate_b, value, d_cgate, x, d_res, gains, conv, pieces
):
    rows, width = d_conv.shape
    block = row_block(rows)
    steps = rows // block
    wide = by_rows(block, width)
    narrow = by_rows(block, 1)
    count = len(pieces)
    ahead = lambda i: (jnp.minimum((i + 1) * (block // 16), rows // 16 - 1), 0)
    return pl.pallas_call(
        functools.partial(mixer_last_kernel, count, steps),
        grid=(steps,),
        in_specs=[
            pl.BlockSpec(memory_space=pltpu.SMEM),
            wide,
            pl.BlockSpec((16, width), ahead),
            whole(after),
            narrow,
            pl.BlockSpec((16, 1), ahead),
            narrow,
        ]
        + [wide] * 3
        + [whole(gains), whole(conv)]
        + [by_rows(block, v.shape[1]) for v in gate_b + value]
        + [units(v, 0, 3) for v in pieces],
        out_specs=[wide] * 3 + [pl.BlockSpec((8, width), lambda i: (0, 0))],
        out_shape=[
            struct(rows, width, BF16),
            struct(rows, width, BF16),
            struct(rows, width, F32),
            struct(8, width, F32),
        ],
        compiler_params=params(),
        cost_estimate=cost(),
        name="mixer_last",
    )(
        mask, d_conv, d_conv, after, keep, keep, keep_after,
        d_cgate, x, d_res, gains, conv, *gate_b, *value, *pieces,
    )


def body(
    tokens,
    starts,
    norm_gains,
    in_weight,
    conv_weight,
    out_weight,
    ffn_weight,
    down_weight,
    cotangent,
):
    row_count, width = tokens.shape
    count = lax.axis_size("tensor")
    dp_count = lax.axis_size("dp")
    here = lax.axis_index("tensor")
    rows = row_count // count
    first = here * rows

    keep_all = 1.0 - starts.astype(F32)
    edge = jnp.concatenate(
        [tokens[-HEAD:], jnp.broadcast_to(keep_all[-1], (HEAD, width)).astype(BF16)], 0
    )
    before = shift(edge, "dp", 1)
    back = jnp.maximum(first - HEAD, 0)
    head_rows = jnp.where(
        here == 0, before[:HEAD], lax.dynamic_slice_in_dim(tokens, back, HEAD, 0)
    )
    keep_prev = jnp.where(
        here == 0,
        before[HEAD, 0].astype(F32),
        lax.dynamic_index_in_dim(keep_all, jnp.maximum(first - 1, 0), 0, False),
    )
    keep = lax.dynamic_slice_in_dim(keep_all, first, rows, 0)
    keep_before = jnp.concatenate([keep_prev[None], keep[:-1]])[:, None]
    keep_after = jnp.concatenate([keep[1:], jnp.ones((1,), F32)])[:, None]
    keep = keep[:, None]

    packed = jnp.concatenate([in_weight, out_weight.T[None]], 0)
    pieces = [packed, swap(packed, "tensor", 1)]
    conv = [conv_weight] + [swap(conv_weight, "tensor", k) for k in range(1, count)]
    conv = jnp.concatenate(conv, 1)
    x_share = lax.dynamic_slice_in_dim(tokens, first, rows, 0)
    x_ext = jnp.concatenate([head_rows, x_share], 0)
    x_ext, keep, keep_before, keep_after, conv = lax.optimization_barrier(
        (x_ext, keep, keep_before, keep_after, conv)
    )
    g_all, d_act = act_grad(here, count, cotangent, down_weight)

    channels = width // count
    *part, resid, normed = mixer_forward(
        after(x_ext, d_act), keep, keep_before, norm_gains, conv[:, : 2 * channels],
        pieces, None, False,
    )
    normed_in = normed
    saved = [part]
    for k in range(2, count, 2):
        far_pieces = gather_far(packed, k, d_act, resid)
        pieces = pieces + far_pieces
        *part, resid = mixer_forward(
            x_ext, keep, keep_before, norm_gains, conv[:, k * channels : (k + 2) * channels],
            far_pieces, resid, k == count - 2,
        )
        if k == count - 2:
            normed_ffn = resid
            resid = part.pop()
        saved.append(part)
    gate_b, gate_c, value, mixed, one, two, gated_mix = [list(v) for v in zip(*saved)]

    near = swap(normed_ffn, "tensor", 1)
    far = {k: swap(normed_ffn, "tensor", k) for k in range(2, count, 2)}
    *held, block_a, block_b, dnf_a, dnf_b = ffn(
        normed_ffn, near, d_act, ffn_weight, down_weight, 0, 0, 2, ()
    )
    own = (dnf_a, swap(dnf_b, "tensor", 1), block_a, swap(block_b, "tensor", 1))
    dnf_far = {}
    dnf_sent = {}
    block_far = {}
    for k in range(2, count, 2):
        nf_a = after(far[k], block_a)
        if k == 2:
            gated_all = jnp.concatenate(gated_mix, 1)
            own = lax.optimization_barrier(own + (nf_a, gated_all))
            gated_all = own[5]
            dnf_own = add_low(own[0], own[1])
            block_own = add_low(own[2], own[3])
        *held, block_a, block_b, dnf_a, dnf_b = ffn(
            nf_a, swap(nf_a, "tensor", 1), after(d_act, dnf_own, block_own), ffn_weight, down_weight, k, 0, 2, held
        )
        dnf_sent[k] = add_low(dnf_a, swap(dnf_b, "tensor", 1))
        dnf_far[k] = swap(dnf_sent[k], "tensor", k)
        block_far[k] = (block_a, swap(block_b, "tensor", 1))
    nf_all, act, d_gu = held
    block_sent = {k: add_low(*block_far[k]) for k in range(2, count, 2)}
    bits = dp_bits()

    grad_down = matmul(g_all, after(act, *dnf_sent.values()), OUTER).astype(BF16)
    d_gu = after(d_gu, grad_down)
    grad_gate = matmul(nf_all, d_gu[0], OUTER).astype(BF16)
    d_up = after(d_gu[1], grad_gate, *dnf_far.values())
    grad_up = matmul(nf_all, d_up, OUTER).astype(BF16)
    ffn_grads = lax.psum_scatter(
        jnp.stack([grad_gate, grad_up, grad_down]), "dp", scatter_dimension=1, tiled=True
    ).astype(F32)

    d_nf = [dnf_own] + [after(dnf_far[k], grad_up, block_sent[k]) for k in range(2, count, 2)]
    d_res, d_res_low, d_cgate, d_conv, sums, edge_back = mixer_middle(
        g_all, resid, norm_gains, conv, keep, d_nf, gate_c, mixed, one, two, pieces
    )
    back_edge = shift(edge_back, ("dp", "tensor"), -1)
    first, first_sent = mixer_grad([normed_in, d_res_low], [d_cgate, gated_all], count)
    first_sent = swap(first_sent, "tensor", 1)
    received = after(back_edge, first)
    mask = (here ^ ((here + 1) % count)).astype(jnp.int32)[None]
    d_b, d_v, grad_tokens, gain_one = mixer_last(
        mask, d_conv, received, keep, keep_after, gate_b, value, d_cgate, x_share, d_res,
        norm_gains, conv, pieces,
    )
    first = chip_sums(first, after(first_sent, d_b))
    first_far = [swap(first[k // 2], "tensor", k) for k in range(2, count, 2)]
    second, second_sent = mixer_grad([normed_in], [after(d_b, first[0]), d_v], count)
    second = chip_sums(second, swap(second_sent, "tensor", 1))
    second_far = [swap(second[k // 2], "tensor", k) for k in range(2, count, 2)]
    small = jnp.concatenate([gain_one[:1], sums[3:4], to_owners(sums[:3])], 0)
    flat = (dp_count, -1, channels)

    def chip_total(group, far, *deps):
        far = lax.optimization_barrier(tuple(far) + deps)[: len(far)]
        sent, kept = fold(
            group[0].reshape(flat), [v.reshape(flat) for v in far], low_to=1, to_bits=1
        )
        return kept, None, swap(sent, "dp", 1), bits[1:]

    first = chip_total(first, first_far, second[0])
    second = chip_total(second, second_far, first[0])
    small = after(small, second[0])
    low = 1
    while low < count:
        small = small + swap(small, "tensor", low)
        low *= 2
    block_far = {k: swap(after(block_sent[k], small), "tensor", k) for k in block_sent}
    while first[3]:
        first = step(first, first[3][0], second[0])
        second = step(second, second[3][0], first[0])
    block_sum = block_own.astype(F32)
    for k in range(2, count, 2):
        block_sum = block_sum + after(block_far[k], first[0]).astype(F32)
    block_out = (resid + block_sum).astype(BF16)
    for low in bits:
        small = small + swap(small, "dp", low)
    first = close(first)[0]
    second = close(second)[0]
    out_c, out_o = first.reshape(2, -1, channels)
    out_b, out_v = second.reshape(2, -1, channels)
    return (
        block_out,
        grad_tokens,
        small[:2],
        jnp.stack([out_b, out_c, out_v]),
        small[2:],
        out_o.T,
        ffn_grads[:2],
        ffn_grads[2].T,
    )


def solution(mesh):
    return jax.shard_map(
        body,
        mesh=mesh,
        in_specs=(
            P("dp", None),
            P("dp"),
            P(),
            P(None, None, "tensor"),
            P(None, "tensor"),
            P("tensor", None),
            P(None, None, "tensor"),
            P("tensor", None),
            P("dp", None),
        ),
        out_specs=(
            P(("dp", "tensor"), None),
            P(("dp", "tensor"), None),
            P(),
            P(None, "dp", "tensor"),
            P(),
            P("tensor", "dp"),
            P(None, "dp", "tensor"),
            P("tensor", "dp"),
        ),
        check_vma=False,
    )
```
